32 devices in a mesh: groups: 2 (over y), dp: 8 (over z, x), tensor: 2 (over core).
Axes of the slice: x: 2, y: 2, z: 4, core: 2. Of those that a mesh axis runs over, the one named last changes fastest.
Arguments:
- xbc: bfloat16 [2048, 9216], P(('groups', 'dp', 'tensor')), parts along dimension 0, may hold values from -6 to 6
- gate_z: bfloat16 [2048, 8192], P(('groups', 'dp', 'tensor')), parts along dimension 0, may hold values from -6 to 6
- dt_raw: bfloat16 [2048, 128], P(('groups', 'dp', 'tensor')), parts along dimension 0, may hold values from -6 to 6
- conv_weight: float32 [4, 9216], replicated, may hold values from -3 to 3
- conv_bias: float32 [9216], replicated, may hold values from -3 to 3
- dt_bias: float32 [128], P('tensor'), may hold values from -4 to -1
- decay_rate: float32 [128], P('tensor'), may hold values from 0.02 to 2
- d_skip: float32 [128], P('tensor'), may hold values from 0.5 to 2
- norm_gain: float32 [8192], P('tensor'), may hold values from 0.5 to 1.5
- ssm_store: bfloat16 [16, 128, 64, 128], P(('groups', 'dp'), 'tensor'), parts along dimension 0, may hold values from -1.1953125 to 1.1953125
- conv_store: bfloat16 [16, 3, 9216], P(('groups', 'dp'), None, 'tensor'), parts along dimension 0, may hold values from -6 to 6
- source_of: int32 [16], P('groups'), parts along dimension 0, may hold values from 0 to 7, each once
- prefix_len: int32 [16], P(('groups', 'dp')), parts along dimension 0, may hold values from 0 to 8192, as said below
- span_len: int32 [16], P(('groups', 'dp')), parts along dimension 0, may hold values from 32 to 128
Outputs:
- mixed: bfloat16 [2048, 8192], P(('groups', 'dp'), 'tensor'), parts along dimension 0
The draws below stay inside these ranges and needn't reach their ends.
There are 2 independent parts, one for each index of `groups`. The reference program is written for one: setup_inputs(seed, part) draws one part's arguments, and reference() takes and returns one part's arrays. A program takes and returns all parts, laid end to end along the dimension named above; an argument that names none is the same for every part. Nothing has to cross between parts.
Inputs may be any that keep to these rules, and one draw needn't show every extreme that they name: `source_of`: each of 0 to 7 appears once. `prefix_len`: 0 marks a request without kept states.
All inputs are finite; a program needn't handle non-finite values.
Results may differ from the reference program's by a relative error of at most 0.0045.
Values may be sent and summed in bfloat16 or wider, within the bound.
A program may use at most 64 MiB of HBM per device.

```python
import math
import jax
import jax.numpy as jnp
from jax import lax

HEADS = 128
HEAD_DIM = 64
STATE = 128
GROUPS = 4
NORM_WIDTH = 2048
KCONV = 4
PREFIX_MAX = 8192
TOK_DEV = 128
REQS = 8
TOKENS = 1024
INNER = 8192
CONV_CH = 9216
CONV_HALF = 4608


def draw_prefix_len(key, part):
    key_len, key_fresh = jax.random.split(jax.random.fold_in(key, 11))
    lengths = jax.random.randint(key_len, (REQS,), 1, PREFIX_MAX + 1)
    fresh = jax.random.randint(key_fresh, (REQS,), 0, 4) == 0
    lengths = jnp.where(fresh, 0, lengths)
    index = jnp.arange(REQS)
    lengths = jnp.where(index == 0, PREFIX_MAX, lengths)
    lengths = jnp.where(index == 1, 0, lengths)
    return lengths.astype(jnp.int32)


def draw_span_len(key, part):
    lengths = jax.random.randint(jax.random.fold_in(key, 23), (REQS,), TOK_DEV // 4, TOK_DEV + 1)
    index = jnp.arange(REQS)
    lengths = jnp.where(index == 0, TOK_DEV, lengths)
    return lengths.astype(jnp.int32)


def block_levels(stream_key, dims, cuts, low, top_value):
    def one(position, shards_of):
        heights = jax.random.uniform(jax.random.fold_in(jax.random.fold_in(stream_key, 6), position), (shards_of,), jnp.float32, low / len(cuts), top_value / len(cuts))
        return jnp.repeat(jnp.exp(heights), dims[position] // shards_of).reshape((-1,) + (1,) * (len(dims) - position - 1))

    factor_of = one(*cuts[0])
    for cut in cuts[1:]:
        factor_of = factor_of * one(*cut)
    return factor_of


def scatter_about(own_key, dims, deviation, limit, shards=(), kind=jnp.bfloat16):
    values = jax.random.normal(own_key, dims, jnp.float32) * deviation
    if len(shards) > 0:
        values = block_levels(own_key, dims, shards, -0.22, 0.18) * values
    return jnp.clip(values, min=-limit, max=limit).astype(kind)


def setup_inputs(seed: int = 0, part: int = 0) -> dict:
    seeds = jax.random.split(jax.random.key(seed), 15)
    part_splits = jax.random.split(jax.random.fold_in(seeds[14], part), 15)
    return {
        "xbc": scatter_about(part_splits[0], (TOKENS, CONV_CH), 1.0, 6.0, ((0, 16),)),
        "gate_z": scatter_about(part_splits[1], (TOKENS, INNER), 1.0, 6.0, ((0, 16),)),
        "dt_raw": scatter_about(part_splits[2], (TOKENS, HEADS), 1.0, 6.0, ((0, 16),)),
        "conv_weight": scatter_about(seeds[3], (KCONV, CONV_CH), KCONV ** -0.5, 3.0, (), jnp.float32),
        "conv_bias": scatter_about(seeds[4], (CONV_CH,), 0.5, 3.0, (), jnp.float32),
        "dt_bias": jnp.clip(-4.0 + 3.0 * jax.random.uniform(seeds[5], (HEADS,), jnp.float32) ** block_levels(seeds[5], (HEADS,), ((0, 2),), -0.2, 0.2), -4.0, -1.0),
        "decay_rate": jnp.clip(jnp.exp(math.log(2.0) - 4.6051702 * jax.random.uniform(seeds[6], (HEADS,), jnp.float32) ** block_levels(seeds[6], (HEADS,), ((0, 2),), -0.2, 0.2)), 0.02, 2.0),
        "d_skip": jnp.clip(0.5 + 1.5 * jax.random.uniform(seeds[7], (HEADS,), jnp.float32) ** block_levels(seeds[7], (HEADS,), ((0, 2),), -0.2, 0.2), 0.5, 2.0),
        "norm_gain": jnp.clip(1.0 + 0.1 * jax.random.normal(seeds[8], (INNER,), jnp.float32), 0.5, 1.5),
        "ssm_store": scatter_about(part_splits[9], (REQS, HEADS, HEAD_DIM, STATE), 0.2, 1.1953125, ((0, 8), (1, 2))),
        "conv_store": scatter_about(part_splits[10], (REQS, KCONV - 1, CONV_CH), 1.0, 6.0, ((0, 8), (2, 2))),
        "source_of": jax.random.permutation(part_splits[11], REQS).astype(jnp.int32),
        "prefix_len": draw_prefix_len(jax.random.fold_in(jax.random.fold_in(seeds[14], part), 71), part),
        "span_len": draw_span_len(jax.random.fold_in(jax.random.fold_in(seeds[14], part), 71), part),
    }


EPSILON = 1e-05

def convolve(rims, rows, weight, bias):
    extended = jnp.concatenate([rims, rows], axis=0).astype(jnp.float32)
    count = rows.shape[0]
    total = bias[None, :]
    for offset in range(weight.shape[0]):
        total = total + weight[offset][None, :] * extended[offset:offset + count]
    return jax.nn.silu(total).astype(jnp.bfloat16)

def state_space(activated, gate_rows, dt_rows, dt_bias, decay_rate, d_skip, norm_gain, kept_state, live_rows):
    count = activated.shape[0]
    heads = dt_bias.shape[0]
    inner = heads * HEAD_DIM
    groups = (activated.shape[1] - inner) // (2 * STATE)
    per_group = heads // groups
    x_heads = activated[:, :inner].reshape(count, heads, HEAD_DIM).astype(jnp.float32)
    b_proj = activated[:, inner:inner + groups * STATE].reshape(count, groups, STATE).astype(jnp.float32)
    c_proj = activated[:, inner + groups * STATE:].reshape(count, groups, STATE).astype(jnp.float32)
    step_size = jax.nn.softplus(dt_rows.astype(jnp.float32) + dt_bias[None, :])
    cumulative = jnp.cumsum(-decay_rate[None, :] * step_size, axis=0)
    scores = jnp.einsum('tgn,ugn->gtu', c_proj, b_proj)
    spread = cumulative.T[:, :, None] - cumulative.T[:, None, :]
    causal = jnp.arange(count, dtype=jnp.int32)[:, None] >= jnp.arange(count, dtype=jnp.int32)[None, :]
    decay = jnp.where(causal, jnp.exp(jnp.where(causal, spread, 0.0)), 0.0)
    weights = decay.reshape(groups, per_group, count, count) * scores[:, None] * step_size.T.reshape(groups, per_group, 1, count)
    weights = weights.reshape(heads, count, count).astype(jnp.bfloat16)
    intra = jnp.einsum('htu,uhp->thp', weights.astype(jnp.float32), x_heads)
    state_full = kept_state.astype(jnp.float32).reshape(groups, per_group, HEAD_DIM, STATE)
    carried = jnp.einsum('tgn,gkpn->tgkp', c_proj, state_full)
    carried = carried.reshape(count, heads, HEAD_DIM) * jnp.exp(cumulative)[:, :, None]
    mixed = intra + carried + d_skip[None, :, None] * x_heads
    gated = mixed.reshape(count, inner) * jax.nn.silu(gate_rows.astype(jnp.float32))
    grouped = gated.reshape(count, inner // NORM_WIDTH, NORM_WIDTH)
    scale = lax.rsqrt(lax.optimization_barrier(jnp.mean(grouped * grouped, axis=-1, keepdims=True)) + EPSILON)
    normed = (grouped * scale).reshape(count, inner) * norm_gain[None, :]
    return jnp.where(live_rows[:, None], normed, 0.0).astype(jnp.bfloat16)

def reference(xbc, gate_z, dt_raw, conv_weight, conv_bias, dt_bias, decay_rate, d_skip, norm_gain, ssm_store, conv_store, source_of, prefix_len, span_len):
    x_width = HEADS // 2 * HEAD_DIM
    b_width = GROUPS // 2 * STATE
    xbc_req = xbc.reshape(REQS, TOK_DEV, CONV_CH)
    gate_req = gate_z.reshape(REQS, TOK_DEV, INNER)
    dt_req = dt_raw.reshape(REQS, TOK_DEV, HEADS)

    def reorder(rows):
        halves = rows.reshape(rows.shape[0], 2, CONV_HALF)
        x_part = halves[:, :, :x_width].reshape(rows.shape[0], INNER)
        b_part = halves[:, :, x_width:x_width + b_width].reshape(rows.shape[0], GROUPS * STATE)
        c_part = halves[:, :, x_width + b_width:].reshape(rows.shape[0], GROUPS * STATE)
        return jnp.concatenate([x_part, b_part, c_part], axis=1)

    def serve(index):
        source = source_of[index]
        live = prefix_len[index] > 0
        state = jnp.where(live, ssm_store[source], jnp.zeros_like(ssm_store[source]))
        rims = jnp.where(live, conv_store[source], jnp.zeros_like(conv_store[source]))
        activated = convolve(rims, xbc_req[index], conv_weight, conv_bias)
        live_rows = jnp.arange(TOK_DEV, dtype=jnp.int32) < span_len[index]
        return state_space(reorder(activated), gate_req[index], dt_req[index], dt_bias, decay_rate, d_skip, norm_gain, state, live_rows)
    outputs = lax.map(serve, jnp.arange(REQS, dtype=jnp.int32))
    return outputs.reshape(TOKENS, INNER)
```

```python
import functools
import math

import jax
import jax.numpy as jnp
from jax import lax
from jax.experimental import pallas as pl
from jax.experimental.pallas import tpu as pltpu
from jax.sharding import PartitionSpec as P

HEAD_DIM = 64
STATE = 128
NORM_WIDTH = 2048
LANES = 128
EPSILON = 1e-05
LOG2E = math.log2(math.e)
F32 = jnp.float32
BF16 = jnp.bfloat16
MESH = pl.DeviceIdType.MESH
TRANS_B = (((1,), (1,)), ((), ()))


def each(first, last, body):
    if last - first <= 16:
        for index in range(first, last):
            body(index)
    else:
        lax.fori_loop(first, last, lambda index, carry: (body(index), carry)[1], 0)


def silu(value):
    return 0.5 * value * (1.0 + jnp.tanh(0.5 * value))


def kernel(
    n,
    xbc,
    gate,
    dt,
    weight,
    bias,
    dt_bias,
    decay,
    d_skip,
    gain,
    state,
    conv_store,
    source_of,
    prefix_len,
    span_len,
    out,
    x_all,
    gate_all,
    dt_all,
    w_half,
    b_half,
    rim_f32,
    rim_mine,
    rim_held,
    rim_pick,
    rim_got,
    held,
    pick,
    got,
    ext,
    act,
    cum_roll,
    cum_t,
    step_t,
    score,
    fixed,
    factor,
    rim_send1,
    rim_recv1,
    rim_send2,
    rim_recv2,
    send1,
    recv1,
    send2,
    recv2,
    pair_send,
    pair_recv,
    local_sem,
    own_sem,
):
    me = lax.axis_index("dp")
    core = lax.axis_index("tensor")
    mate = 1 - core
    rows = xbc.shape[0]
    count = x_all.shape[0]
    half = x_all.shape[1]
    inner = gate_all.shape[1]
    chunks, _, piece, _ = pick.shape
    groups = (half - inner) // (2 * STATE)
    rim_count = conv_store.shape[1]
    tiles = half // LANES

    here = pl.ds(pl.multiple_of(core * rows, rows), rows)
    own_x = pl.ds(pl.multiple_of(core * half, LANES), half)
    own_z = pl.ds(pl.multiple_of(core * inner, LANES), inner)
    local = [
        pltpu.make_async_copy(xbc.at[:, own_x], x_all.at[here, :], local_sem.at[0]),
        pltpu.make_async_copy(gate.at[:, own_z], gate_all.at[here, :], local_sem.at[1]),
        pltpu.make_async_copy(dt, dt_all.at[here, :], local_sem.at[2]),
        pltpu.make_async_copy(weight.at[:, own_x], w_half, local_sem.at[3]),
        pltpu.make_async_copy(bias.at[:, own_x], b_half, local_sem.at[4]),
    ]
    for copy in local:
        copy.start()

    def own_state(c):
        begin = pl.multiple_of((c * n + me) * piece, piece)
        return pltpu.make_async_copy(
            state.at[pl.ds(begin, piece), :], held[c].at[me], own_sem.at[c]
        )

    for c in range(chunks):
        own_state(c).start()

    barrier = pltpu.get_barrier_semaphore()

    def greet(step):
        pl.semaphore_signal(
            barrier, inc=1, device_id={"dp": lax.rem(me + step, n)}, device_id_type=MESH
        )

    each(1, n, greet)
    pl.semaphore_signal(barrier, inc=1, device_id={"tensor": mate}, device_id_type=MESH)

    rim_f32[...] = jnp.zeros_like(rim_f32)
    for i in range(rim_count):
        line = conv_store[0, pl.ds(i, 1), :].astype(F32)
        for j in range(tiles):
            rim_f32[pl.ds(i * tiles + j, 1), :] = line[:, j * LANES : (j + 1) * LANES]
    rim_mine[...] = rim_f32[...].astype(BF16).reshape(rim_mine.shape)
    rim_held[me] = rim_mine[me]

    pl.semaphore_wait(barrier, n)

    def rims1(peer, slot):
        return pltpu.make_async_remote_copy(
            src_ref=rim_mine.at[peer],
            dst_ref=rim_held.at[slot],
            send_sem=rim_send1.at[peer],
            recv_sem=rim_recv1.at[slot],
            device_id={"dp": peer},
            device_id_type=MESH,
        )

    def rims2(peer, slot):
        return pltpu.make_async_remote_copy(
            src_ref=rim_pick.at[peer],
            dst_ref=rim_got.at[slot],
            send_sem=rim_send2.at[peer],
            recv_sem=rim_recv2.at[slot],
            device_id={"dp": peer},
            device_id_type=MESH,
        )

    def states1(c, peer, slot):
        begin = pl.multiple_of((c * n + peer) * piece, piece)
        return pltpu.make_async_remote_copy(
            src_ref=state.at[pl.ds(begin, piece), :],
            dst_ref=held[c].at[slot],
            send_sem=send1.at[c, peer],
            recv_sem=recv1.at[c, slot],
            device_id={"dp": peer},
            device_id_type=MESH,
        )

    def states2(c, peer, slot):
        return pltpu.make_async_remote_copy(
            src_ref=pick.at[c, peer],
            dst_ref=got.at[c, slot],
            send_sem=send2.at[c, peer],
            recv_sem=recv2.at[c, slot],
            device_id={"dp": peer},
            device_id_type=MESH,
        )

    def peer_at(step):
        return lax.rem(me + step, n)

    each(1, n, lambda s: rims1(peer_at(s), me).start())

    other_x = pl.ds(pl.multiple_of(mate * half, LANES), half)
    other_z = pl.ds(pl.multiple_of(mate * inner, LANES), inner)

    def pair(index, source, target):
        return pltpu.make_async_remote_copy(
            src_ref=source,
            dst_ref=target,
            send_sem=pair_send.at[index],
            recv_sem=pair_recv.at[index],
            device_id={"tensor": mate},
            device_id_type=MESH,
        )

    exchange = [
        pair(0, dt, dt_all.at[here, :]),
        pair(1, xbc.at[:, other_x], x_all.at[here, :]),
        pair(2, gate.at[:, other_z], gate_all.at[here, :]),
    ]
    for copy in exchange:
        copy.start()
    for c in range(chunks):
        each(1, n, functools.partial(lambda c, s: states1(c, peer_at(s), me).start(), c))

    each(1, n, lambda s: rims1(peer_at(s), peer_at(s)).wait_recv())

    def choose_rims(d):
        rim_pick[d] = rim_held[source_of[d]]

    each(0, n, choose_rims)
    rim_got[me] = rim_pick[me]
    each(1, n, lambda s: rims2(peer_at(s), me).start())

    for copy in local:
        copy.wait()
    for copy in exchange:
        copy.wait()
    both = dt_all[...].astype(F32)
    mine = jnp.where(core == 0, both, pltpu.roll(both, LANES // 2, 1))
    twice = lambda ref: jnp.concatenate([ref[...], ref[...]], axis=1)
    raised = mine + twice(dt_bias)
    step_size = jnp.maximum(raised, 0.0) + jnp.log1p(jnp.exp(-jnp.abs(raised)))
    t_index = lax.broadcasted_iota(jnp.int32, (count, count), 0)
    u_index = lax.broadcasted_iota(jnp.int32, (count, count), 1)
    lower = (t_index >= u_index).astype(F32)
    cum = jnp.dot(
        lower,
        -twice(decay) * step_size,
        precision=lax.Precision.HIGHEST,
        preferred_element_type=F32,
    )
    cum = cum * LOG2E
    cum_roll[...] = cum
    cum_t[...] = cum.T
    step_t[...] = step_size.T
    live = jnp.where(prefix_len[0] > 0, 1.0, 0.0)

    each(1, n, lambda s: rims2(peer_at(s), peer_at(s)).wait_recv())
    rim_f32[...] = rim_got[...].reshape(rim_f32.shape).astype(F32) * live

    width = ext.shape[1]
    per = width // LANES

    def convolve(j, carry):
        columns = pl.ds(pl.multiple_of(j * width, width), width)
        for i in range(rim_count):
            for m in range(per):
                ext[pl.ds(8 - rim_count + i, 1), m * LANES : (m + 1) * LANES] = rim_f32[
                    pl.ds(i * tiles + j * per + m, 1), :
                ]
        ext[pl.ds(8, count), :] = x_all[:, columns].astype(F32)
        total = b_half[:, columns]
        for k in range(rim_count + 1):
            total = total + w_half[pl.ds(k, 1), columns] * ext[pl.ds(8 - rim_count + k, count), :]
        act[:, columns] = silu(total).astype(BF16)
        return carry

    lax.fori_loop(0, half // width, convolve, 0)

    for g in range(groups):
        b_proj = act[:, inner + g * STATE : inner + (g + 1) * STATE]
        c_proj = act[:, inner + (groups + g) * STATE : inner + (groups + g + 1) * STATE]
        score[g] = lax.dot_general(c_proj, b_proj, TRANS_B, preferred_element_type=F32)

    pairs = inner // LANES
    first_head = lax.broadcasted_iota(jnp.int32, (count, LANES), 1) < HEAD_DIM
    causal = t_index >= u_index

    def inside(q, carry):
        columns = pl.ds(pl.multiple_of(q * LANES, LANES), LANES)
        cum_now = cum_roll[...]
        scores = score[q // (pairs // groups)]
        weights = []
        edges = []
        for m in range(2):
            edge = jnp.broadcast_to(cum_now[:, m : m + 1], (count, count))
            spread = edge - cum_t[pl.ds(2 * q + m, 1), :]
            fall = jnp.exp2(jnp.where(causal, spread, -1e30))
            weights.append((fall * scores * step_t[pl.ds(2 * q + m, 1), :]).astype(BF16))
            edges.append(edge)
        cum_roll[...] = pltpu.roll(cum_now, LANES - 2, 1)
        x_now = act[:, columns]
        none = jnp.zeros_like(x_now)
        stacked = jnp.concatenate(
            [jnp.where(first_head, x_now, none), jnp.where(first_head, none, x_now)], axis=0
        )
        intra = jnp.dot(
            jnp.concatenate(weights, axis=1), stacked, preferred_element_type=F32
        )
        skip = jnp.where(first_head, d_skip[2 * q], d_skip[2 * q + 1])
        open_gate = silu(gate_all[:, columns].astype(F32))
        fixed[:, columns] = (intra + skip * x_now.astype(F32)) * open_gate
        carry_in = jnp.exp2(jnp.where(first_head, edges[0], edges[1])) * live
        factor[:, columns] = carry_in * open_gate
        return carry

    def choose(c):
        own_state(c).wait()
        each(1, n, lambda s: states1(c, peer_at(s), peer_at(s)).wait_recv())

        def choose_one(d):
            pick[c, d] = held[c][source_of[d]]

        each(0, n, choose_one)
        got[c, me] = pick[c, me]
        each(1, n, lambda s: states2(c, peer_at(s), me).start())

    per_chunk = pairs // chunks
    for c in range(chunks):
        lax.fori_loop(c * per_chunk, (c + 1) * per_chunk, inside, 0)
        choose(c)

    alive = lax.broadcasted_iota(jnp.int32, (count, 1), 0) < span_len[0]
    block = inner // chunks
    for c in range(chunks):
        c_proj = act[:, inner + (groups + c) * STATE : inner + (groups + c + 1) * STATE]
        each(1, n, lambda s: states2(c, peer_at(s), peer_at(s)).wait_recv())
        kept = got[c].reshape(block, STATE)
        wide = 256
        total = jnp.zeros((count, LANES), F32)
        for b in range(block // wide):
            columns = slice(c * block + b * wide, c * block + (b + 1) * wide)
            carried = lax.dot_general(
                c_proj,
                kept[b * wide : (b + 1) * wide],
                TRANS_B,
                preferred_element_type=F32,
            )
            gated = fixed[:, columns] + carried * factor[:, columns]
            fixed[:, columns] = gated
            square = gated * gated
            for m in range(wide // LANES):
                total = total + square[:, m * LANES : (m + 1) * LANES]
        mean = jnp.sum(total, axis=1, keepdims=True) * (1.0 / block)
        scale = jnp.where(alive, lax.rsqrt(mean + EPSILON), 0.0)
        for b in range(block // wide):
            columns = slice(c * block + b * wide, c * block + (b + 1) * wide)
            out[:, columns] = (fixed[:, columns] * scale * gain[:, columns]).astype(BF16)

    each(1, n, lambda s: rims1(peer_at(s), me).wait_send())
    each(1, n, lambda s: rims2(peer_at(s), me).wait_send())
    for c in range(chunks):
        each(1, n, functools.partial(lambda c, s: states1(c, peer_at(s), me).wait_send(), c))
        each(1, n, functools.partial(lambda c, s: states2(c, peer_at(s), me).wait_send(), c))


def local(
    n,
    xbc,
    gate_z,
    dt_raw,
    conv_weight,
    conv_bias,
    dt_bias,
    decay_rate,
    d_skip,
    norm_gain,
    ssm_store,
    conv_store,
    source_of,
    prefix_len,
    span_len,
):
    rows = xbc.shape[0]
    count = 2 * rows
    half = xbc.shape[1] // 2
    inner = gate_z.shape[1] // 2
    chunks = inner // NORM_WIDTH
    piece = inner // (chunks * n)
    tiles = half // LANES
    rim_piece = 16 * pl.cdiv(conv_store.shape[1] * tiles, 16 * n)
    vmem = pl.BlockSpec(memory_space=pltpu.VMEM)
    smem = pl.BlockSpec(memory_space=pltpu.SMEM)
    hbm = pl.BlockSpec(memory_space=pl.ANY)
    width = 512
    dma = pltpu.SemaphoreType.DMA
    return pl.pallas_call(
        functools.partial(kernel, n),
        out_shape=jax.ShapeDtypeStruct((count, inner), BF16),
        in_specs=[
            hbm, hbm, hbm, hbm, hbm, vmem, vmem, smem, vmem, hbm, vmem, smem, smem, smem,
        ],
        out_specs=vmem,
        scratch_shapes=[
            pltpu.VMEM((count, half), BF16),
            pltpu.VMEM((count, inner), BF16),
            pltpu.VMEM((count, dt_raw.shape[1]), BF16),
            pltpu.VMEM((conv_weight.shape[0], half), F32),
            pltpu.VMEM((1, half), F32),
            pltpu.VMEM((n * rim_piece, LANES), F32),
            pltpu.VMEM((n, rim_piece, LANES), BF16),
            pltpu.VMEM((n, rim_piece, LANES), BF16),
            pltpu.VMEM((n, rim_piece, LANES), BF16),
            pltpu.VMEM((n, rim_piece, LANES), BF16),
            [pltpu.VMEM((n, piece, STATE), BF16) for _ in range(chunks)],
            pltpu.VMEM((chunks, n, piece, STATE), BF16),
            pltpu.VMEM((chunks, n, piece, STATE), BF16),
            pltpu.VMEM((8 + count, width), F32),
            pltpu.VMEM((count, half), BF16),
            pltpu.VMEM((count, LANES), F32),
            pltpu.VMEM((LANES, count), F32),
            pltpu.VMEM((LANES, count), F32),
            pltpu.VMEM(((half - inner) // (2 * STATE), count, count), F32),
            pltpu.VMEM((count, inner), F32),
            pltpu.VMEM((count, inner), F32),
            dma((n,)),
            dma((n,)),
            dma((n,)),
            dma((n,)),
            dma((chunks, n)),
            dma((chunks, n)),
            dma((chunks, n)),
            dma((chunks, n)),
            dma((3,)),
            dma((3,)),
            dma((5,)),
            dma((chunks,)),
        ],
        compiler_params=pltpu.CompilerParams(
            collective_id=0, has_side_effects=True, vmem_limit_bytes=48 * 1024 * 1024
        ),
    )(
        xbc,
        gate_z,
        dt_raw,
        conv_weight,
        conv_bias.reshape(1, -1),
        dt_bias.reshape(1, -1),
        decay_rate.reshape(1, -1),
        d_skip,
        norm_gain.reshape(1, -1),
        ssm_store.reshape(-1, STATE),
        conv_store,
        source_of,
        prefix_len,
        span_len,
    )


def solution(mesh):
    in_specs = (
        P(("groups", "dp", "tensor"), None),
        P(("groups", "dp", "tensor"), None),
        P(("groups", "dp", "tensor"), None),
        P(),
        P(),
        P("tensor"),
        P("tensor"),
        P("tensor"),
        P("tensor"),
        P(("groups", "dp"), "tensor", None, None),
        P(("groups", "dp"), None, "tensor"),
        P("groups"),
        P(("groups", "dp")),
        P(("groups", "dp")),
    )
    out_specs = P(("groups", "dp"), "tensor")
    return jax.shard_map(
        functools.partial(local, mesh.shape["dp"]),
        mesh=mesh,
        in_specs=in_specs,
        out_specs=out_specs,
        check_vma=False,
    )
```

```python
import functools
import math

import jax
import jax.numpy as jnp
from jax import lax
from jax.experimental import pallas as pl
from jax.experimental.pallas import tpu as pltpu
from jax.sharding import PartitionSpec as P

HEAD_DIM = 64
STATE = 128
NORM_WIDTH = 2048
LANES = 128
EPSILON = 1e-05
LOG2E = math.log2(math.e)
F32 = jnp.float32
BF16 = jnp.bfloat16
MESH = pl.DeviceIdType.MESH
TRANS_B = (((1,), (1,)), ((), ()))


def each(first, last, body):
    if last - first <= 16:
        for index in range(first, last):
            body(index)
    else:
        lax.fori_loop(first, last, lambda index, carry: (body(index), carry)[1], 0)


def silu(value):
    return 0.5 * value * (1.0 + jnp.tanh(0.5 * value))


def kernel(
    n,
    xbc,
    gate,
    dt,
    weight,
    bias,
    dt_bias,
    decay,
    d_skip,
    gain,
    state,
    conv_store,
    source_of,
    prefix_len,
    span_len,
    out,
    x_all,
    gate_all,
    dt_all,
    w_half,
    b_half,
    rim_f32,
    rim_mine,
    rim_held,
    rim_pick,
    rim_got,
    held,
    pick,
    got,
    ext,
    act,
    cum_roll,
    cum_t,
    step_t,
    score,
    fixed,
    factor,
    rim_send1,
    rim_recv1,
    rim_send2,
    rim_recv2,
    send1,
    recv1,
    send2,
    recv2,
    pair_send,
    pair_recv,
    local_sem,
    own_sem,
    dt_bias_v,
    decay_v,
    gain_v,
):
    me = lax.axis_index("dp")
    core = lax.axis_index("tensor")
    mate = 1 - core
    rows = xbc.shape[0]
    count = x_all.shape[0]
    half = x_all.shape[1]
    inner = gate_all.shape[1]
    chunks, _, piece, _ = pick.shape
    groups = (half - inner) // (2 * STATE)
    rim_count = conv_store.shape[1]
    tiles = half // LANES

    here = pl.ds(pl.multiple_of(core * rows, rows), rows)
    own_x = pl.ds(pl.multiple_of(core * half, LANES), half)
    own_z = pl.ds(pl.multiple_of(core * inner, LANES), inner)
    local = [
        pltpu.make_async_copy(xbc.at[:, own_x], x_all.at[here, :], local_sem.at[0]),
        pltpu.make_async_copy(gate.at[:, own_z], gate_all.at[here, :], local_sem.at[1]),
        pltpu.make_async_copy(dt, dt_all.at[here, :], local_sem.at[2]),
        pltpu.make_async_copy(weight.at[:, own_x], w_half, local_sem.at[3]),
        pltpu.make_async_copy(bias.at[:, own_x], b_half, local_sem.at[4]),
        pltpu.make_async_copy(dt_bias, dt_bias_v, local_sem.at[5]),
        pltpu.make_async_copy(decay, decay_v, local_sem.at[6]),
        pltpu.make_async_copy(gain, gain_v, local_sem.at[7]),
    ]
    for copy in local:
        copy.start()

    def own_state(c):
        begin = pl.multiple_of((c * n + me) * piece, piece)
        return pltpu.make_async_copy(
            state.at[pl.ds(begin, piece), :], held[c].at[me], own_sem.at[c]
        )

    for c in range(chunks):
        own_state(c).start()

    barrier = pltpu.get_barrier_semaphore()

    def greet(step):
        pl.semaphore_signal(
            barrier, inc=1, device_id={"dp": lax.rem(me + step, n)}, device_id_type=MESH
        )

    each(1, n, greet)
    pl.semaphore_signal(barrier, inc=1, device_id={"tensor": mate}, device_id_type=MESH)

    rim_f32[...] = jnp.zeros_like(rim_f32)
    for i in range(rim_count):
        line = conv_store[0, pl.ds(i, 1), :].astype(F32)
        for j in range(tiles):
            rim_f32[pl.ds(i * tiles + j, 1), :] = line[:, j * LANES : (j + 1) * LANES]
    rim_mine[...] = rim_f32[...].astype(BF16).reshape(rim_mine.shape)
    rim_held[me] = rim_mine[me]

    pl.semaphore_wait(barrier, n)

    def rims1(peer, slot):
        return pltpu.make_async_remote_copy(
            src_ref=rim_mine.at[peer],
            dst_ref=rim_held.at[slot],
            send_sem=rim_send1.at[peer],
            recv_sem=rim_recv1.at[slot],
            device_id={"dp": peer},
            device_id_type=MESH,
        )

    def rims2(peer, slot):
        return pltpu.make_async_remote_copy(
            src_ref=rim_pick.at[peer],
            dst_ref=rim_got.at[slot],
            send_sem=rim_send2.at[peer],
            recv_sem=rim_recv2.at[slot],
            device_id={"dp": peer},
            device_id_type=MESH,
        )

    def states1(c, peer, slot):
        begin = pl.multiple_of((c * n + peer) * piece, piece)
        return pltpu.make_async_remote_copy(
            src_ref=state.at[pl.ds(begin, piece), :],
            dst_ref=held[c].at[slot],
            send_sem=send1.at[c, peer],
            recv_sem=recv1.at[c, slot],
            device_id={"dp": peer},
            device_id_type=MESH,
        )

    def states2(c, peer, slot):
        return pltpu.make_async_remote_copy(
            src_ref=pick.at[c, peer],
            dst_ref=got.at[c, slot],
            send_sem=send2.at[c, peer],
            recv_sem=recv2.at[c, slot],
            device_id={"dp": peer},
            device_id_type=MESH,
        )

    def peer_at(step):
        return lax.rem(me + step, n)

    each(1, n, lambda s: rims1(peer_at(s), me).start())

    other_x = pl.ds(pl.multiple_of(mate * half, LANES), half)
    other_z = pl.ds(pl.multiple_of(mate * inner, LANES), inner)

    def pair(index, source, target):
        return pltpu.make_async_remote_copy(
            src_ref=source,
            dst_ref=target,
            send_sem=pair_send.at[index],
            recv_sem=pair_recv.at[index],
            device_id={"tensor": mate},
            device_id_type=MESH,
        )

    exchange = [
        pair(0, dt, dt_all.at[here, :]),
        pair(1, xbc.at[:, other_x], x_all.at[here, :]),
        pair(2, gate.at[:, other_z], gate_all.at[here, :]),
    ]
    for copy in exchange:
        copy.start()

    def spread_out(c):
        each(1, n, lambda s: states1(c, peer_at(s), me).start())

    spread_out(0)

    each(1, n, lambda s: rims1(peer_at(s), peer_at(s)).wait_recv())

    def choose_rims(d):
        rim_pick[d] = rim_held[source_of[d]]

    each(0, n, choose_rims)
    rim_got[me] = rim_pick[me]
    each(1, n, lambda s: rims2(peer_at(s), me).start())
    for c in range(1, chunks):
        spread_out(c)

    for copy in local:
        copy.wait()
    for copy in exchange:
        copy.wait()
    both = dt_all[...].astype(F32)
    mine = jnp.where(core == 0, both, pltpu.roll(both, LANES // 2, 1))
    twice = lambda ref: jnp.concatenate([ref[...], ref[...]], axis=1)
    raised = mine + twice(dt_bias_v)
    step_size = jnp.maximum(raised, 0.0) + jnp.log1p(jnp.exp(-jnp.abs(raised)))
    t_index = lax.broadcasted_iota(jnp.int32, (count, count), 0)
    u_index = lax.broadcasted_iota(jnp.int32, (count, count), 1)
    lower = (t_index >= u_index).astype(F32)
    cum = jnp.dot(
        lower,
        -twice(decay_v) * step_size,
        precision=lax.Precision.HIGHEST,
        preferred_element_type=F32,
    )
    cum = cum * LOG2E
    cum_roll[...] = cum
    cum_t[...] = cum.T
    step_t[...] = step_size.T
    live = jnp.where(prefix_len[0] > 0, 1.0, 0.0)

    def choose(c):
        own_state(c).wait()
        each(1, n, lambda s: states1(c, peer_at(s), peer_at(s)).wait_recv())

        def choose_one(d):
            pick[c, d] = held[c][source_of[d]]

        each(0, n, choose_one)
        got[c, me] = pick[c, me]
        each(1, n, lambda s: states2(c, peer_at(s), me).start())

    choose(0)

    each(1, n, lambda s: rims2(peer_at(s), peer_at(s)).wait_recv())
    rim_f32[...] = rim_got[...].reshape(rim_f32.shape).astype(F32) * live

    width = ext.shape[1]
    per = width // LANES

    def convolve(j, carry):
        columns = pl.ds(pl.multiple_of(j * width, width), width)
        for i in range(rim_count):
            for m in range(per):
                ext[pl.ds(8 - rim_count + i, 1), m * LANES : (m + 1) * LANES] = rim_f32[
                    pl.ds(i * tiles + j * per + m, 1), :
                ]
        ext[pl.ds(8, count), :] = x_all[:, columns].astype(F32)
        total = b_half[:, columns]
        for k in range(rim_count + 1):
            total = total + w_half[pl.ds(k, 1), columns] * ext[pl.ds(8 - rim_count + k, count), :]
        act[:, columns] = silu(total).astype(BF16)
        return carry

    lax.fori_loop(0, half // width, convolve, 0)

    for g in range(groups):
        b_proj = act[:, inner + g * STATE : inner + (g + 1) * STATE]
        c_proj = act[:, inner + (groups + g) * STATE : inner + (groups + g + 1) * STATE]
        score[g] = lax.dot_general(c_proj, b_proj, TRANS_B, preferred_element_type=F32)

    pairs = inner // LANES
    first_head = lax.broadcasted_iota(jnp.int32, (count, LANES), 1) < HEAD_DIM
    causal = t_index >= u_index

    def inside(q, carry):
        columns = pl.ds(pl.multiple_of(q * LANES, LANES), LANES)
        cum_now = cum_roll[...]
        scores = score[q // (pairs // groups)]
        weights = []
        edges = []
        for m in range(2):
            edge = jnp.broadcast_to(cum_now[:, m : m + 1], (count, count))
            spread = edge - cum_t[pl.ds(2 * q + m, 1), :]
            fall = jnp.exp2(jnp.where(causal, spread, -1e30))
            weights.append((fall * scores * step_t[pl.ds(2 * q + m, 1), :]).astype(BF16))
            edges.append(edge)
        cum_roll[...] = pltpu.roll(cum_now, LANES - 2, 1)
        x_now = act[:, columns]
        none = jnp.zeros_like(x_now)
        stacked = jnp.concatenate(
            [jnp.where(first_head, x_now, none), jnp.where(first_head, none, x_now)], axis=0
        )
        intra = jnp.dot(
            jnp.concatenate(weights, axis=1), stacked, preferred_element_type=F32
        )
        skip = jnp.where(first_head, d_skip[2 * q], d_skip[2 * q + 1])
        open_gate = silu(gate_all[:, columns].astype(F32))
        fixed[:, columns] = (intra + skip * x_now.astype(F32)) * open_gate
        carry_in = jnp.exp2(jnp.where(first_head, edges[0], edges[1])) * live
        factor[:, columns] = carry_in * open_gate
        return carry

    per_chunk = pairs // chunks
    for c in range(chunks):
        lax.fori_loop(c * per_chunk, (c + 1) * per_chunk, inside, 0)
        if c + 1 < chunks:
            choose(c + 1)

    alive = lax.broadcasted_iota(jnp.int32, (count, 1), 0) < span_len[0]
    block = inner // chunks
    for c in range(chunks):
        c_proj = act[:, inner + (groups + c) * STATE : inner + (groups + c + 1) * STATE]
        each(1, n, lambda s: states2(c, peer_at(s), peer_at(s)).wait_recv())
        kept = got[c].reshape(block, STATE)
        wide = 256
        total = jnp.zeros((count, LANES), F32)
        for b in range(block // wide):
            columns = slice(c * block + b * wide, c * block + (b + 1) * wide)
            carried = lax.dot_general(
                c_proj,
                kept[b * wide : (b + 1) * wide],
                TRANS_B,
                preferred_element_type=F32,
            )
            gated = fixed[:, columns] + carried * factor[:, columns]
            fixed[:, columns] = gated
            square = gated * gated
            for m in range(wide // LANES):
                total = total + square[:, m * LANES : (m + 1) * LANES]
        mean = jnp.sum(total, axis=1, keepdims=True) * (1.0 / block)
        scale = jnp.where(alive, lax.rsqrt(mean + EPSILON), 0.0)
        for b in range(block // wide):
            columns = slice(c * block + b * wide, c * block + (b + 1) * wide)
            out[:, columns] = (fixed[:, columns] * scale * gain_v[:, columns]).astype(BF16)

    each(1, n, lambda s: rims1(peer_at(s), me).wait_send())
    each(1, n, lambda s: rims2(peer_at(s), me).wait_send())
    for c in range(chunks):
        each(1, n, functools.partial(lambda c, s: states1(c, peer_at(s), me).wait_send(), c))
        each(1, n, functools.partial(lambda c, s: states2(c, peer_at(s), me).wait_send(), c))


def local(
    n,
    xbc,
    gate_z,
    dt_raw,
    conv_weight,
    conv_bias,
    dt_bias,
    decay_rate,
    d_skip,
    norm_gain,
    ssm_store,
    conv_store,
    source_of,
    prefix_len,
    span_len,
):
    rows = xbc.shape[0]
    count = 2 * rows
    half = xbc.shape[1] // 2
    inner = gate_z.shape[1] // 2
    chunks = inner // NORM_WIDTH
    piece = inner // (chunks * n)
    tiles = half // LANES
    rim_piece = 16 * pl.cdiv(conv_store.shape[1] * tiles, 16 * n)
    vmem = pl.BlockSpec(memory_space=pltpu.VMEM)
    smem = pl.BlockSpec(memory_space=pltpu.SMEM)
    hbm = pl.BlockSpec(memory_space=pl.ANY)
    width = 512
    dma = pltpu.SemaphoreType.DMA
    return pl.pallas_call(
        functools.partial(kernel, n),
        out_shape=jax.ShapeDtypeStruct((count, inner), BF16),
        in_specs=[
            hbm, hbm, hbm, hbm, hbm, hbm, hbm, smem, hbm, hbm, vmem, smem, smem, smem,
        ],
        out_specs=vmem,
        scratch_shapes=[
            pltpu.VMEM((count, half), BF16),
            pltpu.VMEM((count, inner), BF16),
            pltpu.VMEM((count, dt_raw.shape[1]), BF16),
            pltpu.VMEM((conv_weight.shape[0], half), F32),
            pltpu.VMEM((1, half), F32),
            pltpu.VMEM((n * rim_piece, LANES), F32),
            pltpu.VMEM((n, rim_piece, LANES), BF16),
            pltpu.VMEM((n, rim_piece, LANES), BF16),
            pltpu.VMEM((n, rim_piece, LANES), BF16),
            pltpu.VMEM((n, rim_piece, LANES), BF16),
            [pltpu.VMEM((n, piece, STATE), BF16) for _ in range(chunks)],
            pltpu.VMEM((chunks, n, piece, STATE), BF16),
            pltpu.VMEM((chunks, n, piece, STATE), BF16),
            pltpu.VMEM((8 + count, width), F32),
            pltpu.VMEM((count, half), BF16),
            pltpu.VMEM((count, LANES), F32),
            pltpu.VMEM((LANES, count), F32),
            pltpu.VMEM((LANES, count), F32),
            pltpu.VMEM(((half - inner) // (2 * STATE), count, count), F32),
            pltpu.VMEM((count, inner), F32),
            pltpu.VMEM((count, inner), F32),
            dma((n,)),
            dma((n,)),
            dma((n,)),
            dma((n,)),
            dma((chunks, n)),
            dma((chunks, n)),
            dma((chunks, n)),
            dma((chunks, n)),
            dma((3,)),
            dma((3,)),
            dma((8,)),
            dma((chunks,)),
            pltpu.VMEM((1, inner // HEAD_DIM), F32),
            pltpu.VMEM((1, inner // HEAD_DIM), F32),
            pltpu.VMEM((1, inner), F32),
        ],
        compiler_params=pltpu.CompilerParams(
            collective_id=0, has_side_effects=True, vmem_limit_bytes=60 * 1024 * 1024
        ),
    )(
        xbc,
        gate_z,
        dt_raw,
        conv_weight,
        conv_bias.reshape(1, -1),
        dt_bias.reshape(1, -1),
        decay_rate.reshape(1, -1),
        d_skip,
        norm_gain.reshape(1, -1),
        ssm_store.reshape(-1, STATE),
        conv_store,
        source_of,
        prefix_len,
        span_len,
    )


def solution(mesh):
    in_specs = (
        P(("groups", "dp", "tensor"), None),
        P(("groups", "dp", "tensor"), None),
        P(("groups", "dp", "tensor"), None),
        P(),
        P(),
        P("tensor"),
        P("tensor"),
        P("tensor"),
        P("tensor"),
        P(("groups", "dp"), "tensor", None, None),
        P(("groups", "dp"), None, "tensor"),
        P("groups"),
        P(("groups", "dp")),
        P(("groups", "dp")),
    )
    out_specs = P(("groups", "dp"), "tensor")
    return jax.shard_map(
        functools.partial(local, mesh.shape["dp"]),
        mesh=mesh,
        in_specs=in_specs,
        out_specs=out_specs,
        check_vma=False,
    )
```

```python
import functools
import math

import jax
import jax.numpy as jnp
from jax import lax
from jax.experimental import pallas as pl
from jax.experimental.pallas import tpu as pltpu
from jax.sharding import PartitionSpec as P

HEAD_DIM = 64
STATE = 128
NORM_WIDTH = 2048
LANES = 128
EPSILON = 1e-05
LOG2E = math.log2(math.e)
F32 = jnp.float32
BF16 = jnp.bfloat16
MESH = pl.DeviceIdType.MESH
TRANS_B = (((1,), (1,)), ((), ()))


def each(first, last, body):
    if last - first <= 16:
        for index in range(first, last):
            body(index)
    else:
        lax.fori_loop(first, last, lambda index, carry: (body(index), carry)[1], 0)


def silu(value):
    return 0.5 * value * (1.0 + jnp.tanh(0.5 * value))


def kernel(
    n,
    xbc,
    gate,
    dt,
    weight,
    bias,
    dt_bias,
    decay,
    d_skip_h,
    gain,
    state,
    conv_h,
    source_h,
    prefix_h,
    span_h,
    out,
    x_all,
    gate_all,
    dt_all,
    w_half,
    b_half,
    rim_f32,
    rim_mine,
    rim_held,
    rim_pick,
    rim_got,
    held,
    pick,
    got,
    ext,
    act,
    cum_roll,
    cum_t,
    step_t,
    score,
    fixed,
    factor,
    rim_send1,
    rim_recv1,
    rim_send2,
    rim_recv2,
    send1,
    recv1,
    send2,
    recv2,
    pair_send,
    pair_recv,
    local_sem,
    own_sem,
    dt_bias_v,
    decay_v,
    gain_v,
    d_skip,
    source_of,
    prefix_len,
    span_len,
    conv_store,
    small_sem,
):
    me = lax.axis_index("dp")
    core = lax.axis_index("tensor")
    mate = 1 - core
    rows = xbc.shape[0]
    count = x_all.shape[0]
    half = x_all.shape[1]
    inner = gate_all.shape[1]
    chunks, _, piece, _ = pick.shape
    groups = (half - inner) // (2 * STATE)
    rim_count = conv_store.shape[1]
    tiles = half // LANES

    barrier = pltpu.get_barrier_semaphore()

    def greet(step):
        pl.semaphore_signal(
            barrier, inc=1, device_id={"dp": lax.rem(me + step, n)}, device_id_type=MESH
        )

    each(1, n, greet)
    pl.semaphore_signal(barrier, inc=1, device_id={"tensor": mate}, device_id_type=MESH)

    small = [
        pltpu.make_async_copy(conv_h, conv_store, small_sem.at[0]),
        pltpu.make_async_copy(source_h, source_of, small_sem.at[1]),
        pltpu.make_async_copy(d_skip_h, d_skip, small_sem.at[2]),
        pltpu.make_async_copy(prefix_h, prefix_len, small_sem.at[3]),
        pltpu.make_async_copy(span_h, span_len, small_sem.at[4]),
    ]
    for copy in small:
        copy.start()

    here = pl.ds(pl.multiple_of(core * rows, rows), rows)
    own_x = pl.ds(pl.multiple_of(core * half, LANES), half)
    own_z = pl.ds(pl.multiple_of(core * inner, LANES), inner)
    local = [
        pltpu.make_async_copy(xbc.at[:, own_x], x_all.at[here, :], local_sem.at[0]),
        pltpu.make_async_copy(gate.at[:, own_z], gate_all.at[here, :], local_sem.at[1]),
        pltpu.make_async_copy(dt, dt_all.at[here, :], local_sem.at[2]),
        pltpu.make_async_copy(weight.at[:, own_x], w_half, local_sem.at[3]),
        pltpu.make_async_copy(bias.at[:, own_x], b_half, local_sem.at[4]),
        pltpu.make_async_copy(dt_bias, dt_bias_v, local_sem.at[5]),
        pltpu.make_async_copy(decay, decay_v, local_sem.at[6]),
        pltpu.make_async_copy(gain, gain_v, local_sem.at[7]),
    ]
    for copy in local:
        copy.start()

    def own_state(c):
        begin = pl.multiple_of((c * n + me) * piece, piece)
        return pltpu.make_async_copy(
            state.at[pl.ds(begin, piece), :], held[c].at[me], own_sem.at[c]
        )

    for c in range(chunks):
        own_state(c).start()

    rim_f32[...] = jnp.zeros_like(rim_f32)
    for copy in small:
        copy.wait()
    for i in range(rim_count):
        line = conv_store[0, pl.ds(i, 1), :].astype(F32)
        for j in range(tiles):
            rim_f32[pl.ds(i * tiles + j, 1), :] = line[:, j * LANES : (j + 1) * LANES]
    rim_mine[...] = rim_f32[...].astype(BF16).reshape(rim_mine.shape)
    rim_held[me] = rim_mine[me]

    pl.semaphore_wait(barrier, n)

    def rims1(peer, slot):
        return pltpu.make_async_remote_copy(
            src_ref=rim_mine.at[peer],
            dst_ref=rim_held.at[slot],
            send_sem=rim_send1.at[peer],
            recv_sem=rim_recv1.at[slot],
            device_id={"dp": peer},
            device_id_type=MESH,
        )

    def rims2(peer, slot):
        return pltpu.make_async_remote_copy(
            src_ref=rim_pick.at[peer],
            dst_ref=rim_got.at[slot],
            send_sem=rim_send2.at[peer],
            recv_sem=rim_recv2.at[slot],
            device_id={"dp": peer},
            device_id_type=MESH,
        )

    def states1(c, peer, slot):
        begin = pl.multiple_of((c * n + peer) * piece, piece)
        return pltpu.make_async_remote_copy(
            src_ref=state.at[pl.ds(begin, piece), :],
            dst_ref=held[c].at[slot],
            send_sem=send1.at[c, peer],
            recv_sem=recv1.at[c, slot],
            device_id={"dp": peer},
            device_id_type=MESH,
        )

    def states2(c, peer, slot):
        return pltpu.make_async_remote_copy(
            src_ref=pick.at[c, peer],
            dst_ref=got.at[c, slot],
            send_sem=send2.at[c, peer],
            recv_sem=recv2.at[c, slot],
            device_id={"dp": peer},
            device_id_type=MESH,
        )

    bits = n.bit_length() - 1

    def peer_at(step):
        if n & (n - 1):
            return lax.rem(me + step, n)
        flip = (step + 1) // 2 + (step % 2) * (n // 2 - 1)
        peer = 0
        for b in range(bits):
            weight_b = 1 << b
            peer = peer + weight_b * ((me // weight_b + flip // weight_b) % 2)
        return peer

    each(1, n, lambda s: rims1(peer_at(s), me).start())

    other_x = pl.ds(pl.multiple_of(mate * half, LANES), half)
    other_z = pl.ds(pl.multiple_of(mate * inner, LANES), inner)

    def pair(index, source, target):
        return pltpu.make_async_remote_copy(
            src_ref=source,
            dst_ref=target,
            send_sem=pair_send.at[index],
            recv_sem=pair_recv.at[index],
            device_id={"tensor": mate},
            device_id_type=MESH,
        )

    exchange = [
        pair(0, dt, dt_all.at[here, :]),
        pair(1, xbc.at[:, other_x], x_all.at[here, :]),
        pair(2, gate.at[:, other_z], gate_all.at[here, :]),
    ]
    for copy in exchange:
        copy.start()

    def spread_out(c):
        each(1, n, lambda s: states1(c, peer_at(s), me).start())

    spread_out(0)

    each(1, n, lambda s: rims1(peer_at(s), peer_at(s)).wait_recv())

    def choose_rims(d):
        rim_pick[d] = rim_held[source_of[d]]

    each(0, n, choose_rims)
    rim_got[me] = rim_pick[me]
    each(1, n, lambda s: rims2(peer_at(s), me).start())
    for c in range(1, chunks):
        spread_out(c)

    for copy in local:
        copy.wait()
    for copy in exchange:
        copy.wait()
    both = dt_all[...].astype(F32)
    mine = jnp.where(core == 0, both, pltpu.roll(both, LANES // 2, 1))
    twice = lambda ref: jnp.concatenate([ref[...], ref[...]], axis=1)
    raised = mine + twice(dt_bias_v)
    step_size = jnp.maximum(raised, 0.0) + jnp.log1p(jnp.exp(-jnp.abs(raised)))
    t_index = lax.broadcasted_iota(jnp.int32, (count, count), 0)
    u_index = lax.broadcasted_iota(jnp.int32, (count, count), 1)
    lower = (t_index >= u_index).astype(F32)
    cum = jnp.dot(
        lower,
        -twice(decay_v) * step_size,
        precision=lax.Precision.HIGHEST,
        preferred_element_type=F32,
    )
    cum = cum * LOG2E
    cum_roll[...] = cum
    cum_t[...] = cum.T
    step_t[...] = step_size.T
    live = jnp.where(prefix_len[0] > 0, 1.0, 0.0)

    def choose(c):
        own_state(c).wait()
        each(1, n, lambda s: states1(c, peer_at(s), peer_at(s)).wait_recv())

        def choose_one(d):
            pick[c, d] = held[c][source_of[d]]

        each(0, n, choose_one)
        got[c, me] = pick[c, me]
        each(1, n, lambda s: states2(c, peer_at(s), me).start())

    choose(0)

    each(1, n, lambda s: rims2(peer_at(s), peer_at(s)).wait_recv())
    rim_f32[...] = rim_got[...].reshape(rim_f32.shape).astype(F32) * live

    width = ext.shape[1]
    per = width // LANES

    def convolve(j, carry):
        columns = pl.ds(pl.multiple_of(j * width, width), width)
        for i in range(rim_count):
            for m in range(per):
                ext[pl.ds(8 - rim_count + i, 1), m * LANES : (m + 1) * LANES] = rim_f32[
                    pl.ds(i * tiles + j * per + m, 1), :
                ]
        ext[pl.ds(8, count), :] = x_all[:, columns].astype(F32)
        total = b_half[:, columns]
        for k in range(rim_count + 1):
            total = total + w_half[pl.ds(k, 1), columns] * ext[pl.ds(8 - rim_count + k, count), :]
        act[:, columns] = silu(total).astype(BF16)
        return carry

    lax.fori_loop(0, half // width, convolve, 0)

    for g in range(groups):
        b_proj = act[:, inner + g * STATE : inner + (g + 1) * STATE]
        c_proj = act[:, inner + (groups + g) * STATE : inner + (groups + g + 1) * STATE]
        score[g] = lax.dot_general(c_proj, b_proj, TRANS_B, preferred_element_type=F32)

    pairs = inner // LANES
    first_head = lax.broadcasted_iota(jnp.int32, (count, LANES), 1) < HEAD_DIM
    causal = t_index >= u_index

    def inside(q, carry):
        columns = pl.ds(pl.multiple_of(q * LANES, LANES), LANES)
        cum_now = cum_roll[...]
        scores = score[q // (pairs // groups)]
        weights = []
        edges = []
        for m in range(2):
            edge = jnp.broadcast_to(cum_now[:, m : m + 1], (count, count))
            spread = edge - cum_t[pl.ds(2 * q + m, 1), :]
            fall = jnp.exp2(jnp.where(causal, spread, -1e30))
            weights.append((fall * scores * step_t[pl.ds(2 * q + m, 1), :]).astype(BF16))
            edges.append(edge)
        cum_roll[...] = pltpu.roll(cum_now, LANES - 2, 1)
        x_now = act[:, columns]
        none = jnp.zeros_like(x_now)
        stacked = jnp.concatenate(
            [jnp.where(first_head, x_now, none), jnp.where(first_head, none, x_now)], axis=0
        )
        intra = jnp.dot(
            jnp.concatenate(weights, axis=1), stacked, preferred_element_type=F32
        )
        skip = jnp.where(first_head, d_skip[2 * q], d_skip[2 * q + 1])
        open_gate = silu(gate_all[:, columns].astype(F32))
        fixed[:, columns] = (intra + skip * x_now.astype(F32)) * open_gate
        carry_in = jnp.exp2(jnp.where(first_head, edges[0], edges[1])) * live
        factor[:, columns] = carry_in * open_gate
        return carry

    per_chunk = pairs // chunks
    for c in range(chunks):
        lax.fori_loop(c * per_chunk, (c + 1) * per_chunk, inside, 0)
        if c + 1 < chunks:
            choose(c + 1)

    alive = lax.broadcasted_iota(jnp.int32, (count, 1), 0) < span_len[0]
    block = inner // chunks
    for c in range(chunks):
        c_proj = act[:, inner + (groups + c) * STATE : inner + (groups + c + 1) * STATE]
        each(1, n, lambda s: states2(c, peer_at(s), peer_at(s)).wait_recv())
        kept = got[c].reshape(block, STATE)
        wide = 256
        total = jnp.zeros((count, LANES), F32)
        for b in range(block // wide):
            columns = slice(c * block + b * wide, c * block + (b + 1) * wide)
            carried = lax.dot_general(
                c_proj,
                kept[b * wide : (b + 1) * wide],
                TRANS_B,
                preferred_element_type=F32,
            )
            gated = fixed[:, columns] + carried * factor[:, columns]
            fixed[:, columns] = gated
            square = gated * gated
            for m in range(wide // LANES):
                total = total + square[:, m * LANES : (m + 1) * LANES]
        mean = jnp.sum(total, axis=1, keepdims=True) * (1.0 / block)
        scale = jnp.where(alive, lax.rsqrt(mean + EPSILON), 0.0)
        for b in range(block // wide):
            columns = slice(c * block + b * wide, c * block + (b + 1) * wide)
            out[:, columns] = (fixed[:, columns] * scale * gain_v[:, columns]).astype(BF16)

    each(1, n, lambda s: rims1(peer_at(s), me).wait_send())
    each(1, n, lambda s: rims2(peer_at(s), me).wait_send())
    for c in range(chunks):
        each(1, n, functools.partial(lambda c, s: states1(c, peer_at(s), me).wait_send(), c))
        each(1, n, functools.partial(lambda c, s: states2(c, peer_at(s), me).wait_send(), c))


def local(
    n,
    xbc,
    gate_z,
    dt_raw,
    conv_weight,
    conv_bias,
    dt_bias,
    decay_rate,
    d_skip,
    norm_gain,
    ssm_store,
    conv_store,
    source_of,
    prefix_len,
    span_len,
):
    rows = xbc.shape[0]
    count = 2 * rows
    half = xbc.shape[1] // 2
    inner = gate_z.shape[1] // 2
    chunks = inner // NORM_WIDTH
    piece = inner // (chunks * n)
    tiles = half // LANES
    rim_piece = 16 * pl.cdiv(conv_store.shape[1] * tiles, 16 * n)
    vmem = pl.BlockSpec(memory_space=pltpu.VMEM)
    smem = pl.BlockSpec(memory_space=pltpu.SMEM)
    hbm = pl.BlockSpec(memory_space=pltpu.HBM)
    width = 512
    dma = pltpu.SemaphoreType.DMA
    return pl.pallas_call(
        functools.partial(kernel, n),
        out_shape=jax.ShapeDtypeStruct((count, inner), BF16),
        in_specs=[
            hbm, hbm, hbm, hbm, hbm, hbm, hbm, hbm, hbm, hbm, hbm, hbm, hbm, hbm,
        ],
        out_specs=vmem,
        scratch_shapes=[
            pltpu.VMEM((count, half), BF16),
            pltpu.VMEM((count, inner), BF16),
            pltpu.VMEM((count, dt_raw.shape[1]), BF16),
            pltpu.VMEM((conv_weight.shape[0], half), F32),
            pltpu.VMEM((1, half), F32),
            pltpu.VMEM((n * rim_piece, LANES), F32),
            pltpu.VMEM((n, rim_piece, LANES), BF16),
            pltpu.VMEM((n, rim_piece, LANES), BF16),
            pltpu.VMEM((n, rim_piece, LANES), BF16),
            pltpu.VMEM((n, rim_piece, LANES), BF16),
            [pltpu.VMEM((n, piece, STATE), BF16) for _ in range(chunks)],
            pltpu.VMEM((chunks, n, piece, STATE), BF16),
            pltpu.VMEM((chunks, n, piece, STATE), BF16),
            pltpu.VMEM((8 + count, width), F32),
            pltpu.VMEM((count, half), BF16),
            pltpu.VMEM((count, LANES), F32),
            pltpu.VMEM((LANES, count), F32),
            pltpu.VMEM((LANES, count), F32),
            pltpu.VMEM(((half - inner) // (2 * STATE), count, count), F32),
            pltpu.VMEM((count, inner), F32),
            pltpu.VMEM((count, inner), F32),
            dma((n,)),
            dma((n,)),
            dma((n,)),
            dma((n,)),
            dma((chunks, n)),
            dma((chunks, n)),
            dma((chunks, n)),
            dma((chunks, n)),
            dma((3,)),
            dma((3,)),
            dma((8,)),
            dma((chunks,)),
            pltpu.VMEM((1, inner // HEAD_DIM), F32),
            pltpu.VMEM((1, inner // HEAD_DIM), F32),
            pltpu.VMEM((1, inner), F32),
            pltpu.SMEM(d_skip.shape, F32),
            pltpu.SMEM(source_of.shape, jnp.int32),
            pltpu.SMEM(prefix_len.shape, jnp.int32),
            pltpu.SMEM(span_len.shape, jnp.int32),
            pltpu.VMEM(conv_store.shape, BF16),
            dma((5,)),
        ],
        compiler_params=pltpu.CompilerParams(
            collective_id=0, has_side_effects=True, vmem_limit_bytes=60 * 1024 * 1024
        ),
    )(
        xbc,
        gate_z,
        dt_raw,
        conv_weight,
        conv_bias.reshape(1, -1),
        dt_bias.reshape(1, -1),
        decay_rate.reshape(1, -1),
        d_skip,
        norm_gain.reshape(1, -1),
        ssm_store.reshape(-1, STATE),
        conv_store,
        source_of,
        prefix_len,
        span_len,
    )


def solution(mesh):
    in_specs = (
        P(("groups", "dp", "tensor"), None),
        P(("groups", "dp", "tensor"), None),
        P(("groups", "dp", "tensor"), None),
        P(),
        P(),
        P("tensor"),
        P("tensor"),
        P("tensor"),
        P("tensor"),
        P(("groups", "dp"), "tensor", None, None),
        P(("groups", "dp"), None, "tensor"),
        P("groups"),
        P(("groups", "dp")),
        P(("groups", "dp")),
    )
    out_specs = P(("groups", "dp"), "tensor")
    return jax.shard_map(
        functools.partial(local, mesh.shape["dp"]),
        mesh=mesh,
        in_specs=in_specs,
        out_specs=out_specs,
        check_vma=False,
    )
```
